512 devices in a mesh: cp: 128 (over z_hi, y, x), hd: 4 (over z_lo, core).
Axes of the slice: x: 4, y: 8, z: 8 (z_hi: 4, z_lo: 2; z = z_hi * 2 + z_lo), core: 2. Of those that a mesh axis runs over, the one named last changes fastest.
Arguments:
- queries: bfloat16 [98304, 8, 128], P('cp', 'hd'), may hold values from -384 to 384
- keys_values: bfloat16 [2, 98304, 128], P(None, ('cp', 'hd')), may hold values from -32 to 32
- doc_start: int32 [98304], P('cp'), may hold values from 0 to 98303, as said below
Outputs:
- attended: bfloat16 [98304, 8, 128], P('cp', 'hd')
- log_total: float32 [8, 98304], P('hd', 'cp')
The draws below stay inside these ranges and needn't reach their ends.
Inputs may be any that keep to these rules, and one draw needn't show every extreme that they name: doc_start[t] is the first position of the document holding token t; documents are contiguous runs and never cross a boundary between aligned groups of 4 shards of 768 tokens, so a token's document starts at most 3 shards before the token's own shard, and in every draw some document reaches exactly that far.
All inputs are finite; a program needn't handle non-finite values.
Results may differ from the reference program's by a relative error of at most 0.015.
Values may be sent and summed in bfloat16 or wider, within the bound.
No kernel may reach another device: no remote copies, remote signals or barrier semaphores. Data moves between devices by JAX's collectives and lax.ppermute only.
A program may use at most 64 MiB of HBM per device.

```python
import jax
import jax.numpy as jnp
from jax import lax

GROUP_HEADS = 8
HEAD_DIM = 128
TOK_DEV = 768
REACH = 3
TOKENS = 98304
N_CP = 128


def shared_rows(key):
    base_rows = jnp.clip(jax.random.normal(jax.random.fold_in(key, 5), (TOKENS, HEAD_DIM), jnp.float32), -4.0, 4.0)
    return base_rows


def draw_queries(key, part):
    key = jax.random.fold_in(key, 21)
    shape_all = (TOKENS, GROUP_HEADS, HEAD_DIM)
    drawn = jnp.clip(jax.random.normal(jax.random.fold_in(key, 1), shape_all, jnp.float32), -4.0, 4.0)
    return drawn.astype(jnp.bfloat16)


def draw_keys_values(key, part):
    base_rows = shared_rows(key)
    key = jax.random.fold_in(key, 22)
    values = jnp.clip(jax.random.normal(jax.random.fold_in(key, 1), (TOKENS, HEAD_DIM), jnp.float32), -4.0, 4.0)
    key_part = base_rows
    return jnp.stack([key_part, values]).astype(jnp.bfloat16)


def draw_doc_start(key, part):
    key = jax.random.fold_in(key, 31)
    position = jnp.arange(TOKENS, dtype=jnp.int32)
    group_len = (REACH + 1) * TOK_DEV
    group_count = TOKENS // group_len
    long_flag = jax.random.randint(jax.random.fold_in(key, 1), (group_count,), 0, 2)
    long_flag = long_flag.at[0].set(1)
    long_flag = long_flag.at[group_count - 1].set(1)
    tail_len = jax.random.randint(jax.random.fold_in(key, 2), (group_count,), 1, TOK_DEV)
    rolls = jax.random.randint(jax.random.fold_in(key, 3), (TOKENS,), 0, TOK_DEV)
    fresh = rolls < 3
    group_of = position // group_len
    offset = position % group_len
    is_long = long_flag[group_of] == 1
    cut_at = REACH * TOK_DEV + tail_len[group_of]
    boundary = (offset == 0) | (position == TOKENS - 1) | jnp.where(is_long, (offset == cut_at) | fresh & (offset > cut_at), fresh)
    marks = jnp.where(boundary, position, 0)
    return lax.cummax(marks, axis=0).astype(jnp.int32)


def setup_inputs(seed: int = 0) -> dict:
    keys = jax.random.split(jax.random.key(seed), 4)
    return {
        "queries": draw_queries(jax.random.fold_in(keys[3], 71), 0),
        "keys_values": draw_keys_values(jax.random.fold_in(keys[3], 71), 0),
        "doc_start": draw_doc_start(jax.random.fold_in(keys[3], 71), 0),
    }


MASKED_SCORE = -1.0e30


def reference(queries, keys_values, doc_start):
    score_scale = HEAD_DIM ** -0.5
    window_len = (REACH + 1) * TOK_DEV
    front_len = REACH * TOK_DEV
    padded = jnp.concatenate([jnp.zeros((2, front_len, HEAD_DIM), keys_values.dtype), keys_values], axis=1)

    def per_shard(shard_index):
        q_first = (shard_index * TOK_DEV).astype(jnp.int32)
        query_block = lax.dynamic_slice_in_dim(queries, q_first, TOK_DEV, 0).astype(jnp.float32)
        starts = lax.dynamic_slice_in_dim(doc_start, q_first, TOK_DEV, 0).astype(jnp.int32)
        window = lax.dynamic_slice_in_dim(padded, q_first, window_len, 1).astype(jnp.float32)
        q_pos = q_first + jnp.arange(TOK_DEV, dtype=jnp.int32)
        k_pos = q_first - front_len + jnp.arange(window_len, dtype=jnp.int32)
        visible = (k_pos[None, :] <= q_pos[:, None]) & (k_pos[None, :] >= starts[:, None])
        scores = jnp.einsum("qhd,kd->hqk", query_block, window[0]) * score_scale
        scores = jnp.where(visible[None], scores, MASKED_SCORE)
        row_peak = jnp.max(scores, axis=-1)
        weights = jnp.where(visible[None], jnp.exp(scores - row_peak[..., None]), 0.0)
        row_total = jnp.sum(weights, axis=-1)
        rounded = lax.optimization_barrier(weights.astype(jnp.bfloat16))
        weighted = jnp.einsum("hqk,kd->hqd", rounded.astype(jnp.float32), window[1])
        output_block = (weighted / row_total[..., None]).transpose(1, 0, 2).astype(jnp.bfloat16)
        return output_block, row_peak + jnp.log(row_total)

    blocks, logs = lax.map(per_shard, jnp.arange(N_CP, dtype=jnp.int32))
    attended = blocks.reshape(TOKENS, GROUP_HEADS, HEAD_DIM)
    log_total = logs.transpose(1, 0, 2).reshape(GROUP_HEADS, TOKENS)
    return attended, log_total
```

```python
import functools
import math

import jax
import jax.numpy as jnp
from jax import lax
from jax.experimental import pallas as pl
from jax.experimental.pallas import tpu as pltpu
from jax.sharding import Mesh, PartitionSpec as P

GROUP = 4
MASKED_SCORE = -1e30
LOG2E = math.log2(math.e)
LANES = 128


def rows_of(block, tokens, heads):
    return pl.ds(block * tokens * heads, tokens * heads)


def start_columns(starts_ref, cols_ref, heads):
    for j in range(starts_ref.shape[0]):
        row = starts_ref[j : j + 1, :].astype(jnp.float32)
        tall = jnp.transpose(jnp.broadcast_to(row, (LANES, LANES)))
        for h in range(heads):
            cols_ref[pl.ds(j * LANES * heads + h, LANES, stride=heads), :] = tall


def scores_of(q, keys):
    return lax.dot_general(q, keys, (((1,), (1,)), ((), ())), preferred_element_type=jnp.float32)


def with_ones(values):
    return jnp.concatenate([values, jnp.ones_like(values)], axis=1)


def mix(weights, values):
    return lax.dot_general(
        weights.astype(jnp.bfloat16), values, (((1,), (0,)), ((), ())), preferred_element_type=jnp.float32
    )


def own_kernel(heads, tokens, scale, meta_ref, starts_ref, q_ref, kv_ref, peak_ref, acc_ref, cols_ref):
    start_columns(starts_ref, cols_ref, heads)
    factor = scale * LOG2E
    base = meta_ref[0].astype(jnp.float32)
    pieces = kv_ref.shape[0]
    keys = jnp.concatenate([kv_ref[i, 0] for i in range(pieces)], axis=0)
    values = with_ones(jnp.concatenate([kv_ref[i, 1] for i in range(pieces)], axis=0))
    blocks = q_ref.shape[0] // (tokens * heads)
    for i in range(blocks):
        rows = rows_of(i, tokens, heads)
        width = (i + 1) * tokens
        s = scores_of(q_ref[rows, :], keys[:width])
        shape = s.shape
        k_pos = lax.broadcasted_iota(jnp.int32, shape, 1)
        q_pos = i * tokens + lax.broadcasted_iota(jnp.int32, shape, 0) // heads
        cols = jnp.concatenate([cols_ref[rows, :] - base] * (width // LANES), axis=1)
        visible = (k_pos <= q_pos) & (k_pos.astype(jnp.float32) >= cols)
        s = jnp.where(visible, s, MASKED_SCORE)
        peak = jnp.max(s, axis=1, keepdims=True)
        weights = jnp.exp2((s - peak) * factor)
        peak_ref[rows, :] = jnp.broadcast_to(peak, (tokens * heads, LANES))
        acc_ref[rows, :] = mix(weights, values[:width])


def earlier_kernel(
    heads, tokens, scale, meta_ref, firsts_ref, starts_ref, q_ref, far_ref, near_ref, peak_in, acc_in,
    out_ref, log_ref, peak_ref, acc_ref, cols_ref,
):
    start_columns(starts_ref, cols_ref, heads)
    factor = scale * LOG2E
    count = q_ref.shape[0]
    blocks = count // (tokens * heads)
    span = count // heads
    peak_ref[...] = peak_in[...]
    acc_ref[...] = acc_in[...]

    def pieces_of(which, half):
        if which == 1:
            return [near_ref[0, i, half] for i in range(4)]
        if which == 3:
            return [near_ref[1, i, half] for i in range(4)]
        return [far_ref[c, i, half] for c in range(2) for i in range(2)]

    for distance in (1, 2, 3):
        first = meta_ref[0] - distance * span

        def attend(i, masked, distance=distance, first=first):
            keys = jnp.concatenate(pieces_of(distance, 0), axis=0)
            values = with_ones(jnp.concatenate(pieces_of(distance, 1), axis=0))
            rows = rows_of(i, tokens, heads)
            s = scores_of(q_ref[rows, :], keys)
            if masked:
                k_pos = lax.broadcasted_iota(jnp.int32, s.shape, 1).astype(jnp.float32)
                cols = cols_ref[rows, :] - first.astype(jnp.float32)
                cols = jnp.concatenate([cols] * (s.shape[1] // LANES), axis=1)
                s = jnp.where(k_pos >= cols, s, MASKED_SCORE)
            before = peak_ref[rows, :1]
            peak = jnp.maximum(before, jnp.max(s, axis=1, keepdims=True))
            weights = jnp.exp2((s - peak) * factor)
            fade = jnp.exp2((before - peak) * factor)
            peak_ref[rows, :] = jnp.broadcast_to(peak, (tokens * heads, LANES))
            acc_ref[rows, :] = acc_ref[rows, :] * fade + mix(weights, values)

        for i in range(blocks):
            lowest = firsts_ref[i * tokens]
            highest = firsts_ref[(i + 1) * tokens - 1]
            some = lowest < first + span
            clear = highest <= first
            pl.when(clear)(functools.partial(attend, i, False))
            pl.when(some & jnp.logical_not(clear))(functools.partial(attend, i, True))

    total = acc_ref[:, LANES:]
    out_ref[...] = (acc_ref[:, :LANES] / total).astype(out_ref.dtype)
    cols_ref[...] = peak_ref[...] * scale + jnp.log(total)
    eye = lax.broadcasted_iota(jnp.int32, (LANES, LANES), 0) == lax.broadcasted_iota(jnp.int32, (LANES, LANES), 1)
    for h in range(heads):
        for j in range(span // LANES):
            tall = cols_ref[pl.ds(j * LANES * heads + h, LANES, stride=heads), :]
            log_ref[h : h + 1, j * LANES : (j + 1) * LANES] = jnp.sum(
                jnp.where(eye, tall, 0.0), axis=0, keepdims=True
            )


def place(s, z, c):
    return (s * 2 + z) * 2 + c


def permuted(value, source):
    pairs = []
    for s in range(GROUP):
        for z in range(2):
            for c in range(2):
                at = source(s, z, c)
                if at[0] >= 0:
                    pairs.append((place(*at), place(s, z, c)))
    return lax.ppermute(value, ("s", "z", "c"), pairs)


def per_device(queries, keys_values, doc_start):
    span, heads, width = queries.shape
    count = span * heads
    scale = width ** (-0.5)
    tokens = 128
    shard = lax.axis_index("g") * GROUP + lax.axis_index("s")
    meta = (shard * span).astype(jnp.int32).reshape(1)
    flat_q = queries.reshape(count, width)
    starts = doc_start.reshape(span // LANES, LANES)

    own = lax.all_gather(keys_values, ("z", "c"), axis=0)
    half = lax.dynamic_slice_in_dim(own, lax.axis_index("c") * 2, 2, 0)
    near = permuted(own, lambda s, z, c: (s - 1, z, c) if c == 0 else (s - 3, z, c))
    far = permuted(half, lambda s, z, c: (s - 2, z, c))

    smem = pl.BlockSpec(memory_space=pltpu.SMEM)
    vmem = pl.BlockSpec(memory_space=pltpu.VMEM)
    peak, acc = pl.pallas_call(
        functools.partial(own_kernel, heads, tokens, scale),
        out_shape=(
            jax.ShapeDtypeStruct((count, LANES), jnp.float32),
            jax.ShapeDtypeStruct((count, 2 * width), jnp.float32),
        ),
        in_specs=[smem, vmem, vmem, vmem],
        out_specs=(vmem, vmem),
        scratch_shapes=[pltpu.VMEM((count, LANES), jnp.float32)],
        compiler_params=pltpu.CompilerParams(vmem_limit_bytes=32 * 1024 * 1024),
        cost_estimate=pl.CostEstimate(flops=600_000_000, bytes_accessed=4_000_000, transcendentals=700_000),
    )(meta, starts, flat_q, own)

    near = lax.all_gather(near, "c", axis=0)
    far = lax.all_gather(far, "c", axis=0)
    out, log_total = pl.pallas_call(
        functools.partial(earlier_kernel, heads, tokens, scale),
        out_shape=(
            jax.ShapeDtypeStruct((count, width), jnp.bfloat16),
            jax.ShapeDtypeStruct((heads, span), jnp.float32),
        ),
        in_specs=[smem, smem, vmem, vmem, vmem, vmem, vmem, vmem],
        out_specs=(vmem, vmem),
        scratch_shapes=[
            pltpu.VMEM((count, LANES), jnp.float32),
            pltpu.VMEM((count, 2 * width), jnp.float32),
            pltpu.VMEM((count, LANES), jnp.float32),
        ],
        compiler_params=pltpu.CompilerParams(vmem_limit_bytes=32 * 1024 * 1024),
        cost_estimate=pl.CostEstimate(flops=4_000_000_000, bytes_accessed=6_000_000, transcendentals=4_000_000),
    )(meta, doc_start, starts, flat_q, far, near, peak, acc)
    return out.reshape(span, heads, width), log_total


def solution(mesh):
    grid = mesh.devices.reshape(-1, GROUP, 2, 2)
    return jax.shard_map(
        per_device,
        mesh=Mesh(grid, ("g", "s", "z", "c")),
        in_specs=(P(("g", "s"), ("z", "c"), None), P(None, ("g", "s", "z", "c"), None), P(("g", "s"))),
        out_specs=(P(("g", "s"), ("z", "c"), None), P(("z", "c"), ("g", "s"))),
        check_vma=False,
    )
```

```python
import functools
import math

import jax
import jax.numpy as jnp
from jax import lax
from jax.experimental import pallas as pl
from jax.experimental.pallas import tpu as pltpu
from jax.sharding import Mesh, PartitionSpec as P

GROUP = 4
MASKED_SCORE = -1e30
LOG2E = math.log2(math.e)
LANES = 128


def rows_of(block, tokens, heads):
    return pl.ds(block * tokens * heads, tokens * heads)


def start_columns(starts_ref, cols_ref, heads):
    for j in range(starts_ref.shape[0]):
        row = starts_ref[j : j + 1, :].astype(jnp.float32)
        tall = jnp.transpose(jnp.broadcast_to(row, (LANES, LANES)))
        for h in range(heads):
            cols_ref[pl.ds(j * LANES * heads + h, LANES, stride=heads), :] = tall


def scores_of(q, keys):
    return lax.dot_general(q, keys, (((1,), (1,)), ((), ())), preferred_element_type=jnp.float32)


def with_ones(values):
    return jnp.concatenate([values, jnp.ones_like(values)], axis=1)


def mix(weights, values):
    return lax.dot_general(
        weights.astype(jnp.bfloat16), values, (((1,), (0,)), ((), ())), preferred_element_type=jnp.float32
    )


def own_kernel(heads, tokens, scale, meta_ref, starts_ref, q_ref, kv_ref, peak_ref, acc_ref, cols_ref):
    start_columns(starts_ref, cols_ref, heads)
    factor = scale * LOG2E
    base = meta_ref[0].astype(jnp.float32)
    pieces = kv_ref.shape[0]
    keys = jnp.concatenate([kv_ref[i, 0] for i in range(pieces)], axis=0)
    values = with_ones(jnp.concatenate([kv_ref[i, 1] for i in range(pieces)], axis=0))
    blocks = q_ref.shape[0] // (tokens * heads)
    for i in range(blocks):
        rows = rows_of(i, tokens, heads)
        width = (i + 1) * tokens
        s = scores_of(q_ref[rows, :], keys[:width])
        shape = s.shape
        k_pos = lax.broadcasted_iota(jnp.int32, shape, 1)
        q_pos = i * tokens + lax.broadcasted_iota(jnp.int32, shape, 0) // heads
        cols = jnp.concatenate([cols_ref[rows, :] - base] * (width // LANES), axis=1)
        visible = (k_pos <= q_pos) & (k_pos.astype(jnp.float32) >= cols)
        s = jnp.where(visible, s, MASKED_SCORE)
        peak = jnp.max(s, axis=1, keepdims=True)
        weights = jnp.exp2((s - peak) * factor)
        peak_ref[rows, :] = jnp.broadcast_to(peak, (tokens * heads, LANES))
        acc_ref[rows, :] = mix(weights, values[:width])


def merge(rows_total, block, peak_ref, acc_ref, q_ref, keys, values, seen_rows, seen_keys, factor):
    values = with_ones(values)
    for i in range(rows_total // block):
        rows = pl.ds(i * block, block)
        s = scores_of(q_ref[rows, :], keys)
        if seen_keys is not None:
            s = jnp.where(seen_keys, s, MASKED_SCORE)
        seen = i * block + lax.broadcasted_iota(jnp.int32, (block, 1), 0) < seen_rows
        before = peak_ref[rows, :1]
        peak = jnp.where(seen, jnp.maximum(before, jnp.max(s, axis=1, keepdims=True)), before)
        weights = jnp.exp2((s - jnp.where(seen, peak, -MASKED_SCORE)) * factor)
        fade = jnp.exp2((before - peak) * factor)
        peak_ref[rows, :] = jnp.broadcast_to(peak, (block, LANES))
        acc_ref[rows, :] = acc_ref[rows, :] * fade + mix(weights, values)


def earlier_kernel(
    heads, block, scale, meta_ref, firsts_ref, starts_ref, q_ref, far_ref, near_ref, peak_in, acc_in,
    out_ref, log_ref, peak_ref, acc_ref, cols_ref,
):
    del peak_in, acc_in
    factor = scale * LOG2E
    count = q_ref.shape[0]
    span = count // heads
    begin = firsts_ref[0]
    seen_rows = jnp.sum(jnp.where(starts_ref[...] == begin, 1.0, 0.0)).astype(jnp.int32) * heads

    def pieces_of(which, half):
        if which == 1:
            return [near_ref[0, i, half] for i in range(4)]
        if which == 3:
            return [near_ref[1, i, half] for i in range(4)]
        return [far_ref[c, i, half] for c in range(2) for i in range(2)]

    for distance in (1, 2, 3):
        first = meta_ref[0] - distance * span

        def attend(cut, distance=distance, first=first):
            keys = jnp.concatenate(pieces_of(distance, 0), axis=0)
            values = jnp.concatenate(pieces_of(distance, 1), axis=0)
            seen_keys = first + lax.broadcasted_iota(jnp.int32, (1, span), 1) >= begin if cut else None
            merge(count, block, peak_ref, acc_ref, q_ref, keys, values, seen_rows, seen_keys, factor)

        pl.when(begin <= first)(functools.partial(attend, False))
        pl.when((begin > first) & (begin < first + span))(functools.partial(attend, True))

    total = acc_ref[:, LANES:]
    out_ref[...] = (acc_ref[:, :LANES] / total).astype(out_ref.dtype)
    cols_ref[...] = peak_ref[...] * scale + jnp.log(total)
    eye = lax.broadcasted_iota(jnp.int32, (LANES, LANES), 0) == lax.broadcasted_iota(jnp.int32, (LANES, LANES), 1)
    for h in range(heads):
        for j in range(span // LANES):
            tall = cols_ref[pl.ds(j * LANES * heads + h, LANES, stride=heads), :]
            log_ref[h : h + 1, j * LANES : (j + 1) * LANES] = jnp.sum(
                jnp.where(eye, tall, 0.0), axis=0, keepdims=True
            )


def place(s, z, c):
    return (s * 2 + z) * 2 + c


def permuted(value, source):
    pairs = []
    for s in range(GROUP):
        for z in range(2):
            for c in range(2):
                at = source(s, z, c)
                if at[0] >= 0:
                    pairs.append((place(*at), place(s, z, c)))
    return lax.ppermute(value, ("s", "z", "c"), pairs)


def per_device(queries, keys_values, doc_start):
    span, heads, width = queries.shape
    count = span * heads
    scale = width ** (-0.5)
    tokens = 128
    shard = lax.axis_index("g") * GROUP + lax.axis_index("s")
    meta = (shard * span).astype(jnp.int32).reshape(1)
    flat_q = queries.reshape(count, width)
    starts = doc_start.reshape(span // LANES, LANES)

    own = lax.all_gather(keys_values, ("z", "c"), axis=0)
    half = lax.dynamic_slice_in_dim(own, lax.axis_index("c") * 2, 2, 0)
    near = permuted(own, lambda s, z, c: (s - 1, z, c) if c == 0 else (s - 3, z, c))
    far = permuted(half, lambda s, z, c: (s - 2, z, c))

    smem = pl.BlockSpec(memory_space=pltpu.SMEM)
    vmem = pl.BlockSpec(memory_space=pltpu.VMEM)
    peak, acc = pl.pallas_call(
        functools.partial(own_kernel, heads, tokens, scale),
        out_shape=(
            jax.ShapeDtypeStruct((count, LANES), jnp.float32),
            jax.ShapeDtypeStruct((count, 2 * width), jnp.float32),
        ),
        in_specs=[smem, vmem, vmem, vmem],
        out_specs=(vmem, vmem),
        scratch_shapes=[pltpu.VMEM((count, LANES), jnp.float32)],
        compiler_params=pltpu.CompilerParams(vmem_limit_bytes=32 * 1024 * 1024),
        cost_estimate=pl.CostEstimate(flops=600_000_000, bytes_accessed=4_000_000, transcendentals=700_000),
    )(meta, starts, flat_q, own)

    near = lax.all_gather(near, "c", axis=0)
    far = lax.all_gather(far, "c", axis=0)
    out, log_total, _, _ = pl.pallas_call(
        functools.partial(earlier_kernel, heads, 256, scale),
        out_shape=(
            jax.ShapeDtypeStruct((count, width), jnp.bfloat16),
            jax.ShapeDtypeStruct((heads, span), jnp.float32),
            jax.ShapeDtypeStruct((count, LANES), jnp.float32),
            jax.ShapeDtypeStruct((count, 2 * width), jnp.float32),
        ),
        in_specs=[smem, smem, vmem, vmem, vmem, vmem, vmem, vmem],
        out_specs=(vmem, vmem, vmem, vmem),
        input_output_aliases={6: 2, 7: 3},
        scratch_shapes=[pltpu.VMEM((count, LANES), jnp.float32)],
        compiler_params=pltpu.CompilerParams(vmem_limit_bytes=32 * 1024 * 1024),
        cost_estimate=pl.CostEstimate(flops=4_000_000_000, bytes_accessed=6_000_000, transcendentals=4_000_000),
    )(meta, doc_start, starts, flat_q, far, near, peak, acc)
    return out.reshape(span, heads, width), log_total


def solution(mesh):
    grid = mesh.devices.reshape(-1, GROUP, 2, 2)
    return jax.shard_map(
        per_device,
        mesh=Mesh(grid, ("g", "s", "z", "c")),
        in_specs=(P(("g", "s"), ("z", "c"), None), P(None, ("g", "s", "z", "c"), None), P(("g", "s"))),
        out_specs=(P(("g", "s"), ("z", "c"), None), P(("z", "c"), ("g", "s"))),
        check_vma=False,
    )
```

```python
import functools
import math

import jax
import jax.numpy as jnp
from jax import lax
from jax.experimental import pallas as pl
from jax.experimental.pallas import tpu as pltpu
from jax.sharding import Mesh, PartitionSpec as P

GROUP = 4
MASKED_SCORE = -1e30
LOG2E = math.log2(math.e)
LANES = 128


def rows_of(block, tokens, heads):
    return pl.ds(block * tokens * heads, tokens * heads)


def start_columns(starts_ref, cols_ref, heads):
    for j in range(starts_ref.shape[0]):
        row = starts_ref[j : j + 1, :].astype(jnp.float32)
        tall = jnp.transpose(jnp.broadcast_to(row, (LANES, LANES)))
        for h in range(heads):
            cols_ref[pl.ds(j * LANES * heads + h, LANES, stride=heads), :] = tall


def scores_of(q, keys):
    return lax.dot_general(q, keys, (((1,), (1,)), ((), ())), preferred_element_type=jnp.float32)


def with_ones(values):
    return jnp.concatenate([values, jnp.ones_like(values)], axis=1)


def mix(weights, values):
    return lax.dot_general(
        weights.astype(jnp.bfloat16), values, (((1,), (0,)), ((), ())), preferred_element_type=jnp.float32
    )


def own_kernel(heads, tokens, scale, meta_ref, starts_ref, q_ref, kv_ref, peak_ref, acc_ref, first_ref, cols_ref):
    begin = jnp.min(starts_ref[...].astype(jnp.float32))
    first_ref[0] = begin.astype(jnp.int32)
    first_ref[1] = jnp.sum(jnp.where(starts_ref[...].astype(jnp.float32) == begin, 1.0, 0.0)).astype(jnp.int32) * heads
    start_columns(starts_ref, cols_ref, heads)
    factor = scale * LOG2E
    base = meta_ref[0].astype(jnp.float32)
    pieces = kv_ref.shape[0]
    keys = jnp.concatenate([kv_ref[i, 0] for i in range(pieces)], axis=0)
    values = with_ones(jnp.concatenate([kv_ref[i, 1] for i in range(pieces)], axis=0))
    blocks = q_ref.shape[0] // (tokens * heads)
    for i in range(blocks):
        rows = rows_of(i, tokens, heads)
        width = (i + 1) * tokens
        s = scores_of(q_ref[rows, :], keys[:width])
        shape = s.shape
        k_pos = lax.broadcasted_iota(jnp.int32, shape, 1)
        q_pos = i * tokens + lax.broadcasted_iota(jnp.int32, shape, 0) // heads
        cols = jnp.concatenate([cols_ref[rows, :] - base] * (width // LANES), axis=1)
        visible = (k_pos <= q_pos) & (k_pos.astype(jnp.float32) >= cols)
        s = jnp.where(visible, s, MASKED_SCORE)
        peak = jnp.max(s, axis=1, keepdims=True)
        weights = jnp.exp2((s - peak) * factor)
        peak_ref[rows, :] = jnp.broadcast_to(peak, (tokens * heads, LANES))
        acc_ref[rows, :] = mix(weights, values[:width])


def block_sums(rows, block, peak_ref, acc_ref, q_ref, chunks, factor):
    q = q_ref[rows, :]
    before = peak_ref[rows, :1]
    peak = before
    met = []
    for keys, values, seen, seen_keys in chunks:
        s = scores_of(q, keys)
        if seen_keys is not None:
            s = jnp.where(seen_keys, s, MASKED_SCORE)
        peak = jnp.where(seen, jnp.maximum(peak, jnp.max(s, axis=1, keepdims=True)), peak)
        met.append((s, values, seen))
    sums = acc_ref[rows, :] * jnp.exp2((before - peak) * factor)
    weights = [jnp.exp2((s - jnp.where(seen, peak, -MASKED_SCORE)) * factor) for s, _, seen in met]
    mixed = mix(jnp.concatenate(weights, axis=1), jnp.concatenate([v for _, v, _ in met], axis=0))
    return jnp.broadcast_to(peak, (block, LANES)), sums + mixed


def earlier_kernel(
    heads, block, scale, meta_ref, row_ref, first_ref, q_ref, far_ref, over_ref, near_ref, peak_in, acc_in,
    out_ref, log_ref, peak_ref, acc_ref, cols_ref,
):
    del peak_in, acc_in
    factor = scale * LOG2E
    count = q_ref.shape[0]
    span = count // heads
    begin = first_ref[0]
    base = meta_ref[0]

    def shard(distance, which):
        if distance == 2:
            pieces = [r[c, which] for r in (far_ref, over_ref) for c in range(2)]
        else:
            pieces = [near_ref[0 if distance == 1 else 1, i, which] for i in range(4)]
        return jnp.concatenate(pieces, axis=0)

    def seen_rows(rows_first):
        return rows_first + lax.broadcasted_iota(jnp.int32, (block, 1), 0) < first_ref[1]

    def finish(rows, peak, sums):
        total = sums[:, LANES:]
        out_ref[rows, :] = (sums[:, :LANES] / total).astype(out_ref.dtype)
        cols_ref[rows, :] = peak * scale + jnp.log(total)

    whole = begin <= base - (GROUP - 1) * span

    @pl.when(whole)
    def _():
        parts = [(shard(d, 0), with_ones(shard(d, 1))) for d in (1, 2, 3)]
        for i in range(0, count, block):
            rows = pl.ds(i, block)
            chunks = [(keys, values, seen_rows(i), None) for keys, values in parts]
            finish(rows, *block_sums(rows, block, peak_ref, acc_ref, q_ref, chunks, factor))

    @pl.when(jnp.logical_not(whole))
    def _():
        for distance in (1, 2, 3):

            @pl.when(begin < base - (distance - 1) * span)
            def _():
                keys, values = shard(distance, 0), with_ones(shard(distance, 1))
                at = lax.broadcasted_iota(jnp.int32, (1, span), 1)
                if distance == 2:
                    half = span // 2
                    at = jnp.where(at < half, at + row_ref[0] * half, at - row_ref[0] * half)
                seen_keys = base - distance * span + at >= begin
                for i in range(0, count, block):
                    rows = pl.ds(i, block)
                    chunks = [(keys, values, seen_rows(i), seen_keys)]
                    peak, sums = block_sums(rows, block, peak_ref, acc_ref, q_ref, chunks, factor)
                    peak_ref[rows, :] = peak
                    acc_ref[rows, :] = sums

        for i in range(0, count, block):
            rows = pl.ds(i, block)
            finish(rows, peak_ref[rows, :], acc_ref[rows, :])

    eye = lax.broadcasted_iota(jnp.int32, (LANES, LANES), 0) == lax.broadcasted_iota(jnp.int32, (LANES, LANES), 1)
    for h in range(heads):
        for j in range(span // LANES):
            tall = cols_ref[pl.ds(j * LANES * heads + h, LANES, stride=heads), :]
            log_ref[h : h + 1, j * LANES : (j + 1) * LANES] = jnp.sum(
                jnp.where(eye, tall, 0.0), axis=0, keepdims=True
            )


def place(s, z, c):
    return (s * 2 + z) * 2 + c


def permuted(value, source):
    pairs = []
    for s in range(GROUP):
        for z in range(2):
            for c in range(2):
                at = source(s, z, c)
                if at is not None and at[0] >= 0:
                    pairs.append((place(*at), place(s, z, c)))
    return lax.ppermute(value, ("s", "z", "c"), pairs)


def per_device(queries, keys_values, doc_start):
    span, heads, width = queries.shape
    count = span * heads
    scale = width ** (-0.5)
    tokens = 128
    shard = lax.axis_index("g") * GROUP + lax.axis_index("s")
    meta = (shard * span).astype(jnp.int32).reshape(1)
    flat_q = queries.reshape(count, width)
    starts = doc_start.reshape(span // LANES, LANES)

    row = lax.axis_index("z").astype(jnp.int32).reshape(1)
    state = (
        jax.ShapeDtypeStruct((count, LANES), jnp.float32),
        jax.ShapeDtypeStruct((count, 2 * width), jnp.float32),
    )
    smem = pl.BlockSpec(memory_space=pltpu.SMEM)
    vmem = pl.BlockSpec(memory_space=pltpu.VMEM)
    params = pltpu.CompilerParams(vmem_limit_bytes=32 * 1024 * 1024)

    far = permuted(keys_values, lambda s, z, c: (s - 2, z, c))
    own = lax.all_gather(keys_values, ("z", "c"), axis=0)
    own, far = lax.optimization_barrier((own, far))
    near = permuted(own, lambda s, z, c: (s - 1, z, c) if c == 0 else (s - 3, z, c))
    far = lax.all_gather(far, "c", axis=0)
    over = permuted(far, lambda s, z, c: (s, 1 - z, c) if s >= 2 else None)
    peak, acc, first = pl.pallas_call(
        functools.partial(own_kernel, heads, tokens, scale),
        out_shape=(*state, jax.ShapeDtypeStruct((2,), jnp.int32)),
        in_specs=[smem, vmem, vmem, vmem],
        out_specs=(vmem, vmem, smem),
        scratch_shapes=[pltpu.VMEM((count, LANES), jnp.float32)],
        compiler_params=params,
        cost_estimate=pl.CostEstimate(flops=600_000_000, bytes_accessed=4_000_000, transcendentals=700_000),
    )(meta, starts, flat_q, own)
    near = lax.all_gather(near, "c", axis=0)
    out, log_total, _, _ = pl.pallas_call(
        functools.partial(earlier_kernel, heads, 256, scale),
        out_shape=(
            jax.ShapeDtypeStruct((count, width), jnp.bfloat16),
            jax.ShapeDtypeStruct((heads, span), jnp.float32),
            *state,
        ),
        in_specs=[smem, smem, smem] + [vmem] * 6,
        out_specs=(vmem,) * 4,
        input_output_aliases={7: 2, 8: 3},
        scratch_shapes=[pltpu.VMEM((count, LANES), jnp.float32)],
        compiler_params=params,
        cost_estimate=pl.CostEstimate(flops=4_000_000_000, bytes_accessed=6_000_000, transcendentals=4_000_000),
    )(meta, row, first, flat_q, far, over, near, peak, acc)
    return out.reshape(span, heads, width), log_total


def solution(mesh):
    grid = mesh.devices.reshape(-1, GROUP, 2, 2)
    return jax.shard_map(
        per_device,
        mesh=Mesh(grid, ("g", "s", "z", "c")),
        in_specs=(P(("g", "s"), ("z", "c"), None), P(None, ("g", "s", "z", "c"), None), P(("g", "s"))),
        out_specs=(P(("g", "s"), ("z", "c"), None), P(("z", "c"), ("g", "s"))),
        check_vma=False,
    )
```

```python
import functools
import math

import jax
import jax.numpy as jnp
from jax import lax
from jax.experimental import pallas as pl
from jax.experimental.pallas import tpu as pltpu
from jax.sharding import Mesh, PartitionSpec as P

GROUP = 4
MASKED_SCORE = -1e30
LOG2E = math.log2(math.e)
LANES = 128


def starts_kernel(heads, meta_ref, starts_ref, cols_ref, first_ref):
    starts = starts_ref[...].astype(jnp.float32)
    begin = jnp.min(starts)
    first_ref[0] = begin.astype(jnp.int32)
    first_ref[1] = jnp.sum(jnp.where(starts == begin, 1.0, 0.0)).astype(jnp.int32) * heads
    starts = starts - meta_ref[0].astype(jnp.float32)
    for j in range(starts.shape[0]):
        tall = jnp.transpose(jnp.broadcast_to(starts[j : j + 1, :], (LANES, LANES)))
        for h in range(heads):
            cols_ref[pl.ds(j * LANES * heads + h, LANES, stride=heads), :] = tall


def scores_of(q, keys):
    return lax.dot_general(q, keys, (((1,), (1,)), ((), ())), preferred_element_type=jnp.float32)


def with_ones(values):
    return jnp.concatenate([values, jnp.ones_like(values)], axis=1)


def mix(weights, values):
    return lax.dot_general(
        weights.astype(jnp.bfloat16), values, (((1,), (0,)), ((), ())), preferred_element_type=jnp.float32
    )


def own_kernel(heads, scale, cols_ref, q_ref, kv_ref, peak_ref, acc_ref):
    factor = scale * LOG2E
    pieces = kv_ref.shape[0]
    keys = jnp.concatenate([kv_ref[i, 0] for i in range(pieces)], axis=0)
    values = with_ones(jnp.concatenate([kv_ref[i, 1] for i in range(pieces)], axis=0))
    block = LANES * heads
    shape = (block, LANES)
    lane = lax.broadcasted_iota(jnp.int32, shape, 1)
    causal = lane <= lax.broadcasted_iota(jnp.int32, shape, 0) // heads
    blocks = q_ref.shape[0] // block

    def scores(i):
        rows = pl.ds(i * block, block)
        s = scores_of(q_ref[rows, :], keys[: (i + 1) * LANES])
        cols = cols_ref[rows, :]
        parts = []
        for j in range(i + 1):
            visible = (lane + j * LANES).astype(jnp.float32) >= cols
            visible = visible & causal if j == i else visible
            parts.append(jnp.where(visible, s[:, j * LANES : (j + 1) * LANES], MASKED_SCORE))
        return jnp.concatenate(parts, axis=1)

    ahead = scores(0)
    for i in range(blocks):
        rows, s = pl.ds(i * block, block), ahead
        if i + 1 < blocks:
            ahead = scores(i + 1)
        peak = jnp.max(s, axis=1, keepdims=True)
        weights = jnp.exp2((s - peak) * factor)
        peak_ref[rows, :] = jnp.broadcast_to(peak, shape)
        acc_ref[rows, :] = mix(weights, values[: (i + 1) * LANES])


def block_sums(rows, block, peak_ref, acc_ref, s, values, seen, factor):
    before = peak_ref[rows, :1]
    reached = jnp.maximum(before, jnp.max(s, axis=1, keepdims=True))
    peak = jnp.where(seen, reached, before)
    weights = jnp.exp2((s - jnp.where(seen, reached, -MASKED_SCORE)) * factor)
    sums = acc_ref[rows, :] * jnp.exp2((before - peak) * factor) + mix(weights, values)
    return jnp.broadcast_to(peak, (block, LANES)), sums


def earlier_kernel(
    heads, block, scale, meta_ref, row_ref, first_ref, q_ref, far_ref, over_ref, near_ref, peak_in, acc_in,
    out_ref, log_ref, peak_ref, acc_ref, cols_ref,
):
    del peak_in, acc_in
    factor = scale * LOG2E
    count = q_ref.shape[0]
    span = count // heads
    begin = first_ref[0]
    base = meta_ref[0]

    def shard(distance, which):
        if distance == 2:
            pieces = [r[c, which] for r in (far_ref, over_ref) for c in range(2)]
        else:
            pieces = [near_ref[0 if distance == 1 else 1, i, which] for i in range(4)]
        return jnp.concatenate(pieces, axis=0)

    def seen_rows(rows_first):
        return rows_first + lax.broadcasted_iota(jnp.int32, (block, 1), 0) < first_ref[1]

    def finish(rows, peak, sums):
        total = sums[:, LANES:]
        out_ref[rows, :] = (sums[:, :LANES] / total).astype(out_ref.dtype)
        cols_ref[rows, :] = peak * scale + jnp.log(total)

    def attend(distances, seen_keys, done):
        keys = jnp.concatenate([shard(d, 0) for d in distances], axis=0)
        values = jnp.concatenate([with_ones(shard(d, 1)) for d in distances], axis=0)

        def scores(i):
            s = scores_of(q_ref[pl.ds(i, block), :], keys)
            return s if seen_keys is None else jnp.where(seen_keys, s, MASKED_SCORE)

        ahead = scores(0)
        for i in range(0, count, block):
            rows, s = pl.ds(i, block), ahead
            if i + block < count:
                ahead = scores(i + block)
            done(rows, *block_sums(rows, block, peak_ref, acc_ref, s, values, seen_rows(i), factor))

    def keep(rows, peak, sums):
        peak_ref[rows, :] = peak
        acc_ref[rows, :] = sums

    three = begin <= base - 3 * span
    two = begin == base - 2 * span
    pl.when(three)(functools.partial(attend, (1, 2, 3), None, finish))
    pl.when(two)(functools.partial(attend, (1, 2), None, finish))

    @pl.when(jnp.logical_not(three | two))
    def _():
        for distance in (1, 2, 3):

            @pl.when(begin < base - (distance - 1) * span)
            def _():
                at = lax.broadcasted_iota(jnp.int32, (1, span), 1)
                if distance == 2:
                    half = span // 2
                    at = jnp.where(at < half, at + row_ref[0] * half, at - row_ref[0] * half)
                attend((distance,), base - distance * span + at >= begin, keep)

        for i in range(0, count, block):
            rows = pl.ds(i, block)
            finish(rows, peak_ref[rows, :], acc_ref[rows, :])

    eye = lax.broadcasted_iota(jnp.int32, (LANES, LANES), 0) == lax.broadcasted_iota(jnp.int32, (LANES, LANES), 1)
    for h in range(heads):
        for j in range(span // LANES):
            tall = cols_ref[pl.ds(j * LANES * heads + h, LANES, stride=heads), :]
            log_ref[h : h + 1, j * LANES : (j + 1) * LANES] = jnp.sum(
                jnp.where(eye, tall, 0.0), axis=0, keepdims=True
            )


def place(s, z, c):
    return (s * 2 + z) * 2 + c


def permuted(value, source):
    pairs = []
    for s in range(GROUP):
        for z in range(2):
            for c in range(2):
                at = source(s, z, c)
                if at is not None and at[0] >= 0:
                    pairs.append((place(*at), place(s, z, c)))
    return lax.ppermute(value, ("s", "z", "c"), pairs)


def per_device(queries, keys_values, doc_start):
    span, heads, width = queries.shape
    count = span * heads
    scale = width ** (-0.5)
    shard = lax.axis_index("g") * GROUP + lax.axis_index("s")
    meta = (shard * span).astype(jnp.int32).reshape(1)
    flat_q = queries.reshape(count, width)
    starts = doc_start.reshape(span // LANES, LANES)

    row = lax.axis_index("z").astype(jnp.int32).reshape(1)
    state = (
        jax.ShapeDtypeStruct((count, LANES), jnp.float32),
        jax.ShapeDtypeStruct((count, 2 * width), jnp.float32),
    )
    smem = pl.BlockSpec(memory_space=pltpu.SMEM)
    vmem = pl.BlockSpec(memory_space=pltpu.VMEM)
    params = pltpu.CompilerParams(vmem_limit_bytes=32 * 1024 * 1024)

    far = permuted(keys_values, lambda s, z, c: (s - 2, z, c))
    own = lax.all_gather(keys_values, ("z", "c"), axis=0)
    own, far = lax.optimization_barrier((own, far))
    near = permuted(own, lambda s, z, c: (s - 1, z, 1) if c == 0 else (s - 3, z, 0))
    far = lax.all_gather(far, "c", axis=0)
    over = permuted(far, lambda s, z, c: (s, 1 - z, c) if s >= 2 else None)
    starts, far = lax.optimization_barrier((starts, far))
    cols, first = pl.pallas_call(
        functools.partial(starts_kernel, heads),
        out_shape=(state[0], jax.ShapeDtypeStruct((2,), jnp.int32)),
        in_specs=[smem, vmem],
        out_specs=(vmem, smem),
        compiler_params=params,
        cost_estimate=pl.CostEstimate(flops=400_000_000, bytes_accessed=1_000_000, transcendentals=0),
    )(meta, starts)
    peak, acc = pl.pallas_call(
        functools.partial(own_kernel, heads, scale),
        out_shape=state,
        in_specs=[vmem, vmem, vmem],
        out_specs=(vmem, vmem),
        compiler_params=params,
        cost_estimate=pl.CostEstimate(flops=600_000_000, bytes_accessed=4_000_000, transcendentals=700_000),
    )(cols, flat_q, own)
    near = lax.all_gather(near, "c", axis=0)
    out, log_total, _, _ = pl.pallas_call(
        functools.partial(earlier_kernel, heads, 384, scale),
        out_shape=(
            jax.ShapeDtypeStruct((count, width), jnp.bfloat16),
            jax.ShapeDtypeStruct((heads, span), jnp.float32),
            *state,
        ),
        in_specs=[smem, smem, smem] + [vmem] * 6,
        out_specs=(vmem,) * 4,
        input_output_aliases={7: 2, 8: 3},
        scratch_shapes=[pltpu.VMEM((count, LANES), jnp.float32)],
        compiler_params=params,
        cost_estimate=pl.CostEstimate(flops=4_000_000_000, bytes_accessed=6_000_000, transcendentals=4_000_000),
    )(meta, row, first, flat_q, far, over, near, peak, acc)
    return out.reshape(span, heads, width), log_total


def solution(mesh):
    grid = mesh.devices.reshape(-1, GROUP, 2, 2)
    return jax.shard_map(
        per_device,
        mesh=Mesh(grid, ("g", "s", "z", "c")),
        in_specs=(P(("g", "s"), ("z", "c"), None), P(None, ("g", "s", "z", "c"), None), P(("g", "s"))),
        out_specs=(P(("g", "s"), ("z", "c"), None), P(("z", "c"), ("g", "s"))),
        check_vma=False,
    )
```

```python
import functools
import math

import jax
import jax.numpy as jnp
from jax import lax
from jax.experimental import pallas as pl
from jax.experimental.pallas import tpu as pltpu
from jax.sharding import Mesh, PartitionSpec as P

GROUP = 4
MASKED_SCORE = -1e30
LOG2E = math.log2(math.e)
LANES = 128


def starts_kernel(heads, starts_ref, cols_ref, first_ref):
    span = starts_ref.shape[0] * LANES
    base = (lax.axis_index("g") * GROUP + lax.axis_index("s")) * span
    starts = starts_ref[...].astype(jnp.float32)
    begin = jnp.min(starts)
    first_ref[0] = begin.astype(jnp.int32)
    first_ref[1] = jnp.sum(jnp.where(starts == begin, 1.0, 0.0)).astype(jnp.int32) * heads
    first_ref[2] = base
    first_ref[3] = lax.axis_index("z")
    starts = starts - base.astype(jnp.float32)
    for j in range(starts.shape[0]):
        tall = jnp.transpose(jnp.broadcast_to(starts[j : j + 1, :], (LANES, LANES)))
        for h in range(heads):
            cols_ref[pl.ds(j * LANES * heads + h, LANES, stride=heads), :] = tall


def scores_of(q, keys):
    return lax.dot_general(q, keys, (((1,), (1,)), ((), ())), preferred_element_type=jnp.float32)


def with_ones(values):
    return jnp.concatenate([values, jnp.ones_like(values)], axis=1)


def mix(weights, values):
    return lax.dot_general(
        weights.astype(jnp.bfloat16), values, (((1,), (0,)), ((), ())), preferred_element_type=jnp.float32
    )


def own_kernel(heads, scale, cols_ref, q_ref, kv_ref, peak_ref, acc_ref):
    factor = scale * LOG2E
    pieces = kv_ref.shape[0]
    keys = jnp.concatenate([kv_ref[i, 0] for i in range(pieces)], axis=0)
    values = with_ones(jnp.concatenate([kv_ref[i, 1] for i in range(pieces)], axis=0))
    block = LANES * heads
    shape = (block, LANES)
    lane = lax.broadcasted_iota(jnp.int32, shape, 1)
    causal = lane <= lax.broadcasted_iota(jnp.int32, shape, 0) // heads
    blocks = q_ref.shape[0] // block

    def scores(i):
        rows = pl.ds(i * block, block)
        s = scores_of(q_ref[rows, :], keys[: (i + 1) * LANES])
        cols = cols_ref[rows, :]
        parts = []
        for j in range(i + 1):
            visible = (lane + j * LANES).astype(jnp.float32) >= cols
            visible = visible & causal if j == i else visible
            parts.append(jnp.where(visible, s[:, j * LANES : (j + 1) * LANES], MASKED_SCORE))
        return jnp.concatenate(parts, axis=1)

    ahead = scores(0)
    for i in range(blocks):
        rows, s = pl.ds(i * block, block), ahead
        if i + 1 < blocks:
            ahead = scores(i + 1)
        peak = jnp.max(s, axis=1, keepdims=True)
        weights = jnp.exp2((s - peak) * factor)
        peak_ref[rows, :] = jnp.broadcast_to(peak, shape)
        acc_ref[rows, :] = mix(weights, values[: (i + 1) * LANES])


def block_sums(rows, block, peak_ref, acc_ref, s, values, seen, factor):
    before = peak_ref[rows, :1]
    reached = jnp.maximum(before, jnp.max(s, axis=1, keepdims=True))
    peak = jnp.where(seen, reached, before)
    weights = jnp.exp2((s - jnp.where(seen, reached, -MASKED_SCORE)) * factor)
    sums = acc_ref[rows, :] * jnp.exp2((before - peak) * factor) + mix(weights, values)
    return jnp.broadcast_to(peak, (block, LANES)), sums


def row_blocks(count):
    parts, blocks, first = (2, 3, 3, 3, 1), [], 0
    for part in parts:
        blocks.append((first, count * part // sum(parts)))
        first += blocks[-1][1]
    return blocks


def earlier_kernel(
    heads, blocks, scale, first_ref, q_ref, far_ref, over_ref, near_ref, peak_in, acc_in,
    out_ref, log_ref, peak_ref, acc_ref, cols_ref,
):
    del peak_in, acc_in
    factor = scale * LOG2E
    count = q_ref.shape[0]
    span = count // heads
    begin = first_ref[0]
    base = first_ref[2]

    def shard(distance, which):
        if distance == 2:
            pieces = [r[c, which] for r in (far_ref, over_ref) for c in range(2)]
        else:
            pieces = [near_ref[0 if distance == 1 else 1, i, which] for i in range(4)]
        return jnp.concatenate(pieces, axis=0)

    def seen_rows(rows_first, block):
        return rows_first + lax.broadcasted_iota(jnp.int32, (block, 1), 0) < first_ref[1]

    def finish(rows, peak, sums):
        total = sums[:, LANES:]
        out_ref[rows, :] = (sums[:, :LANES] / total).astype(out_ref.dtype)
        cols_ref[rows, :] = peak * scale + jnp.log(total)

    def attend(reach):
        keys = jnp.concatenate([shard(d, 0) for d in range(1, reach + 1)], axis=0)
        values = jnp.concatenate([with_ones(shard(d, 1)) for d in range(1, reach + 1)], axis=0)
        at = lax.broadcasted_iota(jnp.int32, (1, span), 1)
        if reach == 2:
            half = span // 2
            at = jnp.where(at < half, at + first_ref[3] * half, at - first_ref[3] * half)
        seen_keys = base - reach * span + at >= begin
        clear = (reach - 1) * span

        def scores(i, block):
            s = scores_of(q_ref[pl.ds(i, block), :], keys)
            last = jnp.where(seen_keys, s[:, clear:], MASKED_SCORE)
            return jnp.concatenate([s[:, :clear], last], axis=1) if clear else last

        ahead = scores(*blocks[0])
        for n, (i, block) in enumerate(blocks):
            rows, s = pl.ds(i, block), ahead
            if n + 1 < len(blocks):
                ahead = scores(*blocks[n + 1])
            finish(rows, *block_sums(rows, block, peak_ref, acc_ref, s, values, seen_rows(i, block), factor))

    for reach in (1, 2, 3):
        enters = begin < base - (reach - 1) * span
        enters = enters & (begin >= base - reach * span) if reach < 3 else enters
        pl.when(enters)(functools.partial(attend, reach))

    @pl.when(begin >= base)
    def _():
        for i, block in blocks:
            rows = pl.ds(i, block)
            finish(rows, peak_ref[rows, :], acc_ref[rows, :])

    eye = lax.broadcasted_iota(jnp.int32, (LANES, LANES), 0) == lax.broadcasted_iota(jnp.int32, (LANES, LANES), 1)
    for h in range(heads):
        for j in range(span // LANES):
            tall = cols_ref[pl.ds(j * LANES * heads + h, LANES, stride=heads), :]
            log_ref[h : h + 1, j * LANES : (j + 1) * LANES] = jnp.sum(
                jnp.where(eye, tall, 0.0), axis=0, keepdims=True
            )


def place(s, z, c):
    return (s * 2 + z) * 2 + c


def permuted(value, source):
    pairs = []
    for s in range(GROUP):
        for z in range(2):
            for c in range(2):
                at = source(s, z, c)
                if at is not None and at[0] >= 0:
                    pairs.append((place(*at), place(s, z, c)))
    return lax.ppermute(value, ("s", "z", "c"), pairs)


def per_device(queries, keys_values, doc_start):
    span, heads, width = queries.shape
    count = span * heads
    scale = width ** (-0.5)
    flat_q = queries.reshape(count, width)
    starts = doc_start.reshape(span // LANES, LANES)

    state = (
        jax.ShapeDtypeStruct((count, LANES), jnp.float32),
        jax.ShapeDtypeStruct((count, 2 * width), jnp.float32),
    )
    smem = pl.BlockSpec(memory_space=pltpu.SMEM)
    vmem = pl.BlockSpec(memory_space=pltpu.VMEM)
    params = pltpu.CompilerParams(vmem_limit_bytes=32 * 1024 * 1024)

    far = permuted(keys_values, lambda s, z, c: (s - 2, z, c))
    own = lax.all_gather(keys_values, ("z", "c"), axis=0)
    own, far = lax.optimization_barrier((own, far))
    near = permuted(own, lambda s, z, c: (s - 1, z, 1) if c == 0 else (s - 3, z, 0))
    far = lax.all_gather(far, "c", axis=0)
    over = permuted(far, lambda s, z, c: (s, 1 - z, c) if s >= 2 else None)
    starts, far = lax.optimization_barrier((starts, far))
    cols, first = pl.pallas_call(
        functools.partial(starts_kernel, heads),
        out_shape=(state[0], jax.ShapeDtypeStruct((4,), jnp.int32)),
        in_specs=[vmem],
        out_specs=(vmem, smem),
        compiler_params=params,
        cost_estimate=pl.CostEstimate(flops=400_000_000, bytes_accessed=1_000_000, transcendentals=0),
    )(starts)
    peak, acc = pl.pallas_call(
        functools.partial(own_kernel, heads, scale),
        out_shape=state,
        in_specs=[vmem, vmem, vmem],
        out_specs=(vmem, vmem),
        compiler_params=params,
        cost_estimate=pl.CostEstimate(flops=600_000_000, bytes_accessed=4_000_000, transcendentals=700_000),
    )(cols, flat_q, own)
    near = lax.all_gather(near, "c", axis=0)
    out, log_total, _, _ = pl.pallas_call(
        functools.partial(earlier_kernel, heads, row_blocks(count), scale),
        out_shape=(
            jax.ShapeDtypeStruct((count, width), jnp.bfloat16),
            jax.ShapeDtypeStruct((heads, span), jnp.float32),
            *state,
        ),
        in_specs=[smem] + [vmem] * 6,
        out_specs=(vmem,) * 4,
        input_output_aliases={5: 2, 6: 3},
        scratch_shapes=[pltpu.VMEM((count, LANES), jnp.float32)],
        compiler_params=params,
        cost_estimate=pl.CostEstimate(flops=4_000_000_000, bytes_accessed=6_000_000, transcendentals=4_000_000),
    )(first, flat_q, far, over, near, peak, acc)
    return out.reshape(span, heads, width), log_total


def solution(mesh):
    grid = mesh.devices.reshape(-1, GROUP, 2, 2)
    return jax.shard_map(
        per_device,
        mesh=Mesh(grid, ("g", "s", "z", "c")),
        in_specs=(P(("g", "s"), ("z", "c"), None), P(None, ("g", "s", "z", "c"), None), P(("g", "s"))),
        out_specs=(P(("g", "s"), ("z", "c"), None), P(("z", "c"), ("g", "s"))),
        check_vma=False,
    )
```

```python
import functools
import math

import jax
import jax.numpy as jnp
from jax import lax
from jax.experimental import pallas as pl
from jax.experimental.pallas import tpu as pltpu
from jax.sharding import Mesh, PartitionSpec as P

GROUP = 4
MASKED_SCORE = -1e30
LOG2E = math.log2(math.e)
LANES = 128


def starts_kernel(heads, starts_ref, cols_ref, first_ref):
    span = starts_ref.shape[0] * LANES
    base = (lax.axis_index("g") * GROUP + lax.axis_index("s")) * span
    starts = starts_ref[...].astype(jnp.float32)
    first_ref[0] = starts_ref[0, 0]
    first_ref[1] = jnp.sum(jnp.where(starts == starts[:1, :1], 1.0, 0.0)).astype(jnp.int32) * heads
    first_ref[2] = base
    first_ref[3] = lax.axis_index("z")
    starts = starts - base.astype(jnp.float32)
    for j in range(starts.shape[0]):
        tall = jnp.transpose(jnp.broadcast_to(starts[j : j + 1, :], (LANES, LANES)))
        for h in range(heads):
            cols_ref[pl.ds(j * LANES * heads + h, LANES, stride=heads), :] = tall


def scores_of(q, keys):
    return lax.dot_general(q, keys, (((1,), (1,)), ((), ())), preferred_element_type=jnp.float32)


def with_ones(values):
    return jnp.concatenate([values, jnp.ones_like(values)], axis=1)


def mix(weights, values):
    return lax.dot_general(
        weights.astype(jnp.bfloat16), values, (((1,), (0,)), ((), ())), preferred_element_type=jnp.float32
    )


def own_kernel(heads, scale, cols_ref, q_ref, kv_ref, peak_ref, acc_ref):
    factor = scale * LOG2E
    pieces = kv_ref.shape[0]
    keys = jnp.concatenate([kv_ref[i, 0] for i in range(pieces)], axis=0)
    values = with_ones(jnp.concatenate([kv_ref[i, 1] for i in range(pieces)], axis=0))
    block = LANES * heads
    shape = (block, LANES)
    lane = lax.broadcasted_iota(jnp.int32, shape, 1)
    causal = lane <= lax.broadcasted_iota(jnp.int32, shape, 0) // heads
    blocks = q_ref.shape[0] // block

    def scores(i):
        rows = pl.ds(i * block, block)
        s = scores_of(q_ref[rows, :], keys[: (i + 1) * LANES])
        cols = cols_ref[rows, :]
        parts = []
        for j in range(i + 1):
            visible = (lane + j * LANES).astype(jnp.float32) >= cols
            visible = visible & causal if j == i else visible
            parts.append(jnp.where(visible, s[:, j * LANES : (j + 1) * LANES], MASKED_SCORE))
        return jnp.concatenate(parts, axis=1)

    ahead = scores(blocks - 1)
    for i in reversed(range(blocks)):
        rows, s = pl.ds(i * block, block), ahead
        if i:
            ahead = scores(i - 1)
        peak = jnp.max(s, axis=1, keepdims=True)
        weights = jnp.exp2((s - peak) * factor)
        peak_ref[rows, :] = jnp.broadcast_to(peak, shape)
        acc_ref[rows, :] = mix(weights, values[: (i + 1) * LANES])


def block_sums(rows, block, peak_ref, acc_ref, s, values, seen, factor):
    before = peak_ref[rows, :1]
    reached = jnp.maximum(before, jnp.max(s, axis=1, keepdims=True))
    peak = jnp.where(seen, reached, before)
    weights = jnp.exp2((s - jnp.where(seen, reached, -MASKED_SCORE)) * factor)
    sums = acc_ref[rows, :] * jnp.exp2((before - peak) * factor) + mix(weights, values)
    return jnp.broadcast_to(peak, (block, LANES)), sums


def row_blocks(count):
    parts, blocks, first = (2, 3, 3, 3, 1), [], 0
    for part in parts:
        blocks.append((first, count * part // sum(parts)))
        first += blocks[-1][1]
    return blocks


def earlier_kernel(
    heads, blocks, scale, first_ref, q_ref, far_ref, over_ref, near_ref, peak_in, acc_in,
    out_ref, log_ref, peak_ref, acc_ref, cols_ref,
):
    del peak_in, acc_in
    factor = scale * LOG2E
    count = q_ref.shape[0]
    span = count // heads
    begin = first_ref[0]
    base = first_ref[2]

    def shard(distance, which):
        if distance == 2:
            pieces = [r[c, which] for r in (far_ref, over_ref) for c in range(2)]
        else:
            pieces = [near_ref[0 if distance == 1 else 1, i, which] for i in range(4)]
        return jnp.concatenate(pieces, axis=0)

    def seen_rows(rows_first, block):
        return rows_first + lax.broadcasted_iota(jnp.int32, (block, 1), 0) < first_ref[1]

    def finish(rows, peak, sums):
        total = sums[:, LANES:]
        out_ref[rows, :] = (sums[:, :LANES] / total).astype(out_ref.dtype)
        cols_ref[rows, :] = peak * scale + jnp.log(total)

    def attend(reach):
        keys = jnp.concatenate([shard(d, 0) for d in range(1, reach + 1)], axis=0)
        values = jnp.concatenate([with_ones(shard(d, 1)) for d in range(1, reach + 1)], axis=0)
        at = lax.broadcasted_iota(jnp.int32, (1, span), 1)
        if reach == 2:
            half = span // 2
            at = jnp.where(at < half, at + first_ref[3] * half, at - first_ref[3] * half)
        seen_keys = base - reach * span + at >= begin
        clear = (reach - 1) * span

        def scores(i, block):
            s = scores_of(q_ref[pl.ds(i, block), :], keys)
            last = jnp.where(seen_keys, s[:, clear:], MASKED_SCORE)
            return jnp.concatenate([s[:, :clear], last], axis=1) if clear else last

        ahead = scores(*blocks[0])
        for n, (i, block) in enumerate(blocks):
            rows, s = pl.ds(i, block), ahead
            if n + 1 < len(blocks):
                ahead = scores(*blocks[n + 1])
            finish(rows, *block_sums(rows, block, peak_ref, acc_ref, s, values, seen_rows(i, block), factor))

    for reach in (1, 2, 3):
        enters = begin < base - (reach - 1) * span
        enters = enters & (begin >= base - reach * span) if reach < 3 else enters
        pl.when(enters)(functools.partial(attend, reach))

    @pl.when(begin >= base)
    def _():
        for i, block in blocks:
            rows = pl.ds(i, block)
            finish(rows, peak_ref[rows, :], acc_ref[rows, :])

    eye = lax.broadcasted_iota(jnp.int32, (LANES, LANES), 0) == lax.broadcasted_iota(jnp.int32, (LANES, LANES), 1)
    for h in range(heads):
        for j in range(span // LANES):
            tall = cols_ref[pl.ds(j * LANES * heads + h, LANES, stride=heads), :]
            log_ref[h : h + 1, j * LANES : (j + 1) * LANES] = jnp.sum(
                jnp.where(eye, tall, 0.0), axis=0, keepdims=True
            )


def place(s, z, c):
    return (s * 2 + z) * 2 + c


def permuted(value, source):
    pairs = []
    for s in range(GROUP):
        for z in range(2):
            for c in range(2):
                at = source(s, z, c)
                if at is not None and at[0] >= 0:
                    pairs.append((place(*at), place(s, z, c)))
    return lax.ppermute(value, ("s", "z", "c"), pairs)


def per_device(queries, keys_values, doc_start):
    span, heads, width = queries.shape
    count = span * heads
    scale = width ** (-0.5)
    flat_q = queries.reshape(count, width)
    starts = doc_start.reshape(span // LANES, LANES)

    state = (
        jax.ShapeDtypeStruct((count, LANES), jnp.float32),
        jax.ShapeDtypeStruct((count, 2 * width), jnp.float32),
    )
    smem = pl.BlockSpec(memory_space=pltpu.SMEM)
    vmem = pl.BlockSpec(memory_space=pltpu.VMEM)
    params = pltpu.CompilerParams(vmem_limit_bytes=32 * 1024 * 1024)

    far = permuted(keys_values, lambda s, z, c: (s - 2, z, c))
    own = lax.all_gather(keys_values, ("z", "c"), axis=0)
    own, far = lax.optimization_barrier((own, far))
    near = permuted(own, lambda s, z, c: (s - 1, z, c) if c == 0 else (s - 3, z, c))
    far = lax.all_gather(far, "c", axis=0)
    over = permuted(far, lambda s, z, c: (s, 1 - z, c) if s >= 2 else None)
    starts, far = lax.optimization_barrier((starts, far))
    cols, first = pl.pallas_call(
        functools.partial(starts_kernel, heads),
        out_shape=(state[0], jax.ShapeDtypeStruct((4,), jnp.int32)),
        in_specs=[vmem],
        out_specs=(vmem, smem),
        compiler_params=params,
        cost_estimate=pl.CostEstimate(flops=400_000_000, bytes_accessed=1_000_000, transcendentals=0),
    )(starts)
    peak, acc = pl.pallas_call(
        functools.partial(own_kernel, heads, scale),
        out_shape=state,
        in_specs=[vmem, vmem, vmem],
        out_specs=(vmem, vmem),
        compiler_params=params,
        cost_estimate=pl.CostEstimate(flops=600_000_000, bytes_accessed=4_000_000, transcendentals=700_000),
    )(cols, flat_q, own)
    near = lax.all_gather(near, "c", axis=0)
    out, log_total, _, _ = pl.pallas_call(
        functools.partial(earlier_kernel, heads, row_blocks(count), scale),
        out_shape=(
            jax.ShapeDtypeStruct((count, width), jnp.bfloat16),
            jax.ShapeDtypeStruct((heads, span), jnp.float32),
            *state,
        ),
        in_specs=[smem] + [vmem] * 6,
        out_specs=(vmem,) * 4,
        input_output_aliases={5: 2, 6: 3},
        scratch_shapes=[pltpu.VMEM((count, LANES), jnp.float32)],
        compiler_params=params,
        cost_estimate=pl.CostEstimate(flops=4_000_000_000, bytes_accessed=6_000_000, transcendentals=4_000_000),
    )(first, flat_q, far, over, near, peak, acc)
    return out.reshape(span, heads, width), log_total


def solution(mesh):
    grid = mesh.devices.reshape(-1, GROUP, 2, 2)
    return jax.shard_map(
        per_device,
        mesh=Mesh(grid, ("g", "s", "z", "c")),
        in_specs=(P(("g", "s"), ("z", "c"), None), P(None, ("g", "s", "z", "c"), None), P(("g", "s"))),
        out_specs=(P(("g", "s"), ("z", "c"), None), P(("z", "c"), ("g", "s"))),
        check_vma=False,
    )
```

```python
import functools
import math

import jax
import jax.numpy as jnp
from jax import lax
from jax.experimental import pallas as pl
from jax.experimental.pallas import tpu as pltpu
from jax.sharding import Mesh, PartitionSpec as P

GROUP = 4
MASKED_SCORE = -1e30
LOG2E = math.log2(math.e)
LANES = 128


def starts_kernel(heads, starts_ref, cols_ref, first_ref):
    span = starts_ref.shape[0] * LANES
    base = (lax.axis_index("g") * GROUP + lax.axis_index("s")) * span
    starts = starts_ref[...].astype(jnp.float32)
    first_ref[0] = starts_ref[0, 0]
    first_ref[1] = jnp.sum(jnp.where(starts == starts[:1, :1], 1.0, 0.0)).astype(jnp.int32) * heads
    first_ref[2] = base
    first_ref[3] = lax.axis_index("z")
    starts = starts - base.astype(jnp.float32)
    for j in range(starts.shape[0]):
        tall = jnp.transpose(jnp.broadcast_to(starts[j : j + 1, :], (LANES, LANES)))
        for h in range(heads):
            cols_ref[pl.ds(j * LANES * heads + h, LANES, stride=heads), :] = tall


def scores_of(q, keys):
    return lax.dot_general(q, keys, (((1,), (1,)), ((), ())), preferred_element_type=jnp.float32)


def with_ones(values):
    return jnp.concatenate([values, jnp.ones_like(values)], axis=1)


def mix(weights, values):
    return lax.dot_general(
        weights.astype(jnp.bfloat16), values, (((1,), (0,)), ((), ())), preferred_element_type=jnp.float32
    )


def own_kernel(heads, scale, cols_ref, q_ref, kv_ref, peak_ref, acc_ref):
    factor = scale * LOG2E
    pieces = kv_ref.shape[0]
    keys = jnp.concatenate([kv_ref[i, 0] for i in range(pieces)], axis=0)
    values = with_ones(jnp.concatenate([kv_ref[i, 1] for i in range(pieces)], axis=0))
    block = LANES * heads
    shape = (block, LANES)
    lane = lax.broadcasted_iota(jnp.int32, shape, 1)
    causal = lane <= lax.broadcasted_iota(jnp.int32, shape, 0) // heads
    blocks = q_ref.shape[0] // block

    def scores(i):
        rows = pl.ds(i * block, block)
        s = scores_of(q_ref[rows, :], keys[: (i + 1) * LANES])
        cols = cols_ref[rows, :]
        parts = []
        for j in range(i + 1):
            visible = (lane + j * LANES).astype(jnp.float32) >= cols
            visible = visible & causal if j == i else visible
            parts.append(jnp.where(visible, s[:, j * LANES : (j + 1) * LANES], MASKED_SCORE))
        return jnp.concatenate(parts, axis=1)

    ahead = scores(blocks - 1)
    for i in reversed(range(blocks)):
        rows, s = pl.ds(i * block, block), ahead
        if i:
            ahead = scores(i - 1)
        peak = jnp.max(s, axis=1, keepdims=True)
        weights = jnp.exp2((s - peak) * factor)
        peak_ref[rows, :] = jnp.broadcast_to(peak, shape)
        acc_ref[rows, :] = mix(weights, values[: (i + 1) * LANES])


def block_sums(rows, block, peak_ref, acc_ref, s, values, seen, factor):
    before = peak_ref[rows, :1]
    reached = jnp.maximum(before, jnp.max(s, axis=1, keepdims=True))
    peak = jnp.where(seen, reached, before)
    weights = jnp.exp2((s - jnp.where(seen, reached, -MASKED_SCORE)) * factor)
    sums = acc_ref[rows, :] * jnp.exp2((before - peak) * factor) + mix(weights, values)
    return jnp.broadcast_to(peak, (block, LANES)), sums


def row_blocks(count):
    parts, blocks, first = (2, 3, 3, 3, 1), [], 0
    for part in parts:
        blocks.append((first, count * part // sum(parts)))
        first += blocks[-1][1]
    return blocks


def earlier_kernel(
    heads, blocks, scale, first_ref, q_ref, far_ref, over_ref, near_ref, peak_ref, acc_ref,
    out_ref, log_ref, cols_ref,
):
    factor = scale * LOG2E
    count = q_ref.shape[0]
    span = count // heads
    begin = first_ref[0]
    base = first_ref[2]

    def shard(distance, which):
        if distance == 2:
            pieces = [r[c, which] for r in (far_ref, over_ref) for c in range(2)]
        else:
            pieces = [near_ref[0 if distance == 1 else 1, i, which] for i in range(4)]
        return jnp.concatenate(pieces, axis=0)

    def seen_rows(rows_first, block):
        return rows_first + lax.broadcasted_iota(jnp.int32, (block, 1), 0) < first_ref[1]

    def finish(rows, peak, sums):
        total = sums[:, LANES:]
        out_ref[rows, :] = (sums[:, :LANES] / total).astype(out_ref.dtype)
        cols_ref[rows, :] = peak * scale + jnp.log(total)

    def attend(reach):
        keys = jnp.concatenate([shard(d, 0) for d in range(1, reach + 1)], axis=0)
        values = jnp.concatenate([with_ones(shard(d, 1)) for d in range(1, reach + 1)], axis=0)
        at = lax.broadcasted_iota(jnp.int32, (1, span), 1)
        if reach == 2:
            half = span // 2
            at = jnp.where(at < half, at + first_ref[3] * half, at - first_ref[3] * half)
        seen_keys = base - reach * span + at >= begin
        clear = (reach - 1) * span

        def scores(i, block):
            s = scores_of(q_ref[pl.ds(i, block), :], keys)
            last = jnp.where(seen_keys, s[:, clear:], MASKED_SCORE)
            return jnp.concatenate([s[:, :clear], last], axis=1) if clear else last

        ahead = scores(*blocks[0])
        for n, (i, block) in enumerate(blocks):
            rows, s = pl.ds(i, block), ahead
            if n + 1 < len(blocks):
                ahead = scores(*blocks[n + 1])
            finish(rows, *block_sums(rows, block, peak_ref, acc_ref, s, values, seen_rows(i, block), factor))

    for reach in (1, 2, 3):
        enters = begin < base - (reach - 1) * span
        enters = enters & (begin >= base - reach * span) if reach < 3 else enters
        pl.when(enters)(functools.partial(attend, reach))

    @pl.when(begin >= base)
    def _():
        for i, block in blocks:
            rows = pl.ds(i, block)
            finish(rows, peak_ref[rows, :], acc_ref[rows, :])

    eye = lax.broadcasted_iota(jnp.int32, (LANES, LANES), 0) == lax.broadcasted_iota(jnp.int32, (LANES, LANES), 1)
    for h in range(heads):
        for j in range(span // LANES):
            tall = cols_ref[pl.ds(j * LANES * heads + h, LANES, stride=heads), :]
            log_ref[h : h + 1, j * LANES : (j + 1) * LANES] = jnp.sum(
                jnp.where(eye, tall, 0.0), axis=0, keepdims=True
            )


def place(s, z, c):
    return (s * 2 + z) * 2 + c


def permuted(value, source):
    pairs = []
    for s in range(GROUP):
        for z in range(2):
            for c in range(2):
                at = source(s, z, c)
                if at is not None and at[0] >= 0:
                    pairs.append((place(*at), place(s, z, c)))
    return lax.ppermute(value, ("s", "z", "c"), pairs)


def per_device(queries, keys_values, doc_start):
    span, heads, width = queries.shape
    count = span * heads
    scale = width ** (-0.5)
    flat_q = queries.reshape(count, width)
    starts = doc_start.reshape(span // LANES, LANES)

    state = (
        jax.ShapeDtypeStruct((count, LANES), jnp.float32),
        jax.ShapeDtypeStruct((count, 2 * width), jnp.float32),
    )
    smem = pl.BlockSpec(memory_space=pltpu.SMEM)
    vmem = pl.BlockSpec(memory_space=pltpu.VMEM)
    params = pltpu.CompilerParams(vmem_limit_bytes=32 * 1024 * 1024)

    far = permuted(keys_values, lambda s, z, c: (s - 2, z, c))
    own = lax.all_gather(keys_values, ("z", "c"), axis=0)
    own, far = lax.optimization_barrier((own, far))
    near = permuted(own, lambda s, z, c: (s - 1, z, c) if c == 0 else (s - 3, z, c))
    far = lax.all_gather(far, "c", axis=0)
    over = permuted(far, lambda s, z, c: (s, 1 - z, c) if s >= 2 else None)
    starts, far = lax.optimization_barrier((starts, far))
    cols, first = pl.pallas_call(
        functools.partial(starts_kernel, heads),
        out_shape=(state[0], jax.ShapeDtypeStruct((4,), jnp.int32)),
        in_specs=[vmem],
        out_specs=(vmem, smem),
        compiler_params=params,
        cost_estimate=pl.CostEstimate(flops=400_000_000, bytes_accessed=1_000_000, transcendentals=0),
    )(starts)
    peak, acc = pl.pallas_call(
        functools.partial(own_kernel, heads, scale),
        out_shape=state,
        in_specs=[vmem, vmem, vmem],
        out_specs=(vmem, vmem),
        compiler_params=params,
        cost_estimate=pl.CostEstimate(flops=600_000_000, bytes_accessed=4_000_000, transcendentals=700_000),
    )(cols, flat_q, own)
    near = lax.all_gather(near, "c", axis=0)
    out, log_total = pl.pallas_call(
        functools.partial(earlier_kernel, heads, row_blocks(count), scale),
        out_shape=(
            jax.ShapeDtypeStruct((count, width), jnp.bfloat16),
            jax.ShapeDtypeStruct((heads, span), jnp.float32),
        ),
        in_specs=[smem] + [vmem] * 6,
        out_specs=(vmem,) * 2,
        scratch_shapes=[pltpu.VMEM((count, LANES), jnp.float32)],
        compiler_params=params,
        cost_estimate=pl.CostEstimate(flops=4_000_000_000, bytes_accessed=6_000_000, transcendentals=4_000_000),
    )(first, flat_q, far, over, near, peak, acc)
    return out.reshape(span, heads, width), log_total


def solution(mesh):
    grid = mesh.devices.reshape(-1, GROUP, 2, 2)
    return jax.shard_map(
        per_device,
        mesh=Mesh(grid, ("g", "s", "z", "c")),
        in_specs=(P(("g", "s"), ("z", "c"), None), P(None, ("g", "s", "z", "c"), None), P(("g", "s"))),
        out_specs=(P(("g", "s"), ("z", "c"), None), P(("z", "c"), ("g", "s"))),
        check_vma=False,
    )
```

```python
import functools
import math

import jax
import jax.numpy as jnp
from jax import lax
from jax.experimental import pallas as pl
from jax.experimental.pallas import tpu as pltpu
from jax.sharding import Mesh, PartitionSpec as P

GROUP = 4
MASKED_SCORE = -1e30
LOG2E = math.log2(math.e)
LANES = 128


def starts_kernel(heads, starts_ref, cols_ref, first_ref):
    span = starts_ref.shape[0] * LANES
    base = (lax.axis_index("g") * GROUP + lax.axis_index("s")) * span
    starts = starts_ref[...].astype(jnp.float32)
    first_ref[0] = starts_ref[0, 0]
    first_ref[1] = jnp.sum(jnp.where(starts == starts[:1, :1], 1.0, 0.0)).astype(jnp.int32) * heads
    first_ref[2] = base
    first_ref[3] = lax.axis_index("z")
    starts = starts - base.astype(jnp.float32)
    for j in range(starts.shape[0]):
        tall = jnp.transpose(jnp.broadcast_to(starts[j : j + 1, :], (LANES, LANES)))
        for h in range(heads):
            cols_ref[pl.ds(j * LANES * heads + h, LANES, stride=heads), :] = tall


def scores_of(q, keys):
    return lax.dot_general(q, keys, (((1,), (1,)), ((), ())), preferred_element_type=jnp.float32)


def with_ones(values):
    return jnp.concatenate([values, jnp.ones_like(values)], axis=1)


def mix(weights, values):
    return lax.dot_general(
        weights.astype(jnp.bfloat16), values, (((1,), (0,)), ((), ())), preferred_element_type=jnp.float32
    )


def own_kernel(heads, scale, cols_ref, q_ref, kv_ref, peak_ref, acc_ref):
    factor = scale * LOG2E
    pieces = kv_ref.shape[0]
    keys = jnp.concatenate([kv_ref[i, 0] for i in range(pieces)], axis=0)
    values = with_ones(jnp.concatenate([kv_ref[i, 1] for i in range(pieces)], axis=0))
    block = LANES * heads
    shape = (block, LANES)
    lane = lax.broadcasted_iota(jnp.int32, shape, 1)
    causal = lane <= lax.broadcasted_iota(jnp.int32, shape, 0) // heads
    blocks = q_ref.shape[0] // block

    def scores(i):
        rows = pl.ds(i * block, block)
        s = scores_of(q_ref[rows, :], keys[: (i + 1) * LANES])
        cols = cols_ref[rows, :]
        parts = []
        for j in range(i + 1):
            visible = (lane + j * LANES).astype(jnp.float32) >= cols
            visible = visible & causal if j == i else visible
            parts.append(jnp.where(visible, s[:, j * LANES : (j + 1) * LANES], MASKED_SCORE))
        return jnp.concatenate(parts, axis=1)

    ahead = scores(blocks - 1)
    for i in reversed(range(blocks)):
        rows, s = pl.ds(i * block, block), ahead
        if i:
            ahead = scores(i - 1)
        peak = jnp.max(s, axis=1, keepdims=True)
        weights = jnp.exp2((s - peak) * factor)
        peak_ref[rows, :] = jnp.broadcast_to(peak, shape)
        acc_ref[rows, :] = mix(weights, values[: (i + 1) * LANES])


def block_sums(rows, block, peak_ref, acc_ref, s, values, seen, factor):
    before = peak_ref[rows, :1]
    reached = jnp.maximum(before, jnp.max(s, axis=1, keepdims=True))
    peak = jnp.where(seen, reached, before)
    weights = jnp.exp2((s - jnp.where(seen, reached, -MASKED_SCORE)) * factor)
    sums = acc_ref[rows, :] * jnp.exp2((before - peak) * factor) + mix(weights, values)
    return jnp.broadcast_to(peak, (block, LANES)), sums


def row_blocks(count):
    parts, blocks, first = (1, 3, 3, 3, 2), [], 0
    for part in parts:
        blocks.append((first, count * part // sum(parts)))
        first += blocks[-1][1]
    return blocks


def earlier_kernel(
    heads, blocks, scale, first_ref, q_ref, far_ref, over_ref, near_ref, peak_ref, acc_ref,
    out_ref, log_ref, cols_ref,
):
    factor = scale * LOG2E
    count = q_ref.shape[0]
    span = count // heads
    begin = first_ref[0]
    base = first_ref[2]

    def shard(distance, which):
        if distance == 2:
            pieces = [r[c, which] for r in (far_ref, over_ref) for c in range(2)]
        else:
            pieces = [near_ref[0 if distance == 1 else 1, i, which] for i in range(4)]
        return jnp.concatenate(pieces, axis=0)

    def seen_rows(rows_first, block):
        return rows_first + lax.broadcasted_iota(jnp.int32, (block, 1), 0) < first_ref[1]

    def finish(rows, peak, sums):
        total = sums[:, LANES:]
        out_ref[rows, :] = (sums[:, :LANES] / total).astype(out_ref.dtype)
        cols_ref[rows, :] = peak * scale + jnp.log(total)

    def attend(reach):
        keys = jnp.concatenate([shard(d, 0) for d in range(1, reach + 1)], axis=0)
        values = jnp.concatenate([with_ones(shard(d, 1)) for d in range(1, reach + 1)], axis=0)
        at = lax.broadcasted_iota(jnp.int32, (1, span), 1)
        if reach == 2:
            half = span // 2
            at = jnp.where(at < half, at + first_ref[3] * half, at - first_ref[3] * half)
        seen_keys = base - reach * span + at >= begin
        clear = (reach - 1) * span

        def scores(i, block):
            s = scores_of(q_ref[pl.ds(i, block), :], keys)
            last = jnp.where(seen_keys, s[:, clear:], MASKED_SCORE)
            return jnp.concatenate([s[:, :clear], last], axis=1) if clear else last

        ahead = scores(*blocks[0])
        for n, (i, block) in enumerate(blocks):
            rows, s = pl.ds(i, block), ahead
            if n + 1 < len(blocks):
                ahead = scores(*blocks[n + 1])
            finish(rows, *block_sums(rows, block, peak_ref, acc_ref, s, values, seen_rows(i, block), factor))

    for reach in (1, 2, 3):
        enters = begin < base - (reach - 1) * span
        enters = enters & (begin >= base - reach * span) if reach < 3 else enters
        pl.when(enters)(functools.partial(attend, reach))

    @pl.when(begin >= base)
    def _():
        for i, block in blocks:
            rows = pl.ds(i, block)
            finish(rows, peak_ref[rows, :], acc_ref[rows, :])

    eye = lax.broadcasted_iota(jnp.int32, (LANES, LANES), 0) == lax.broadcasted_iota(jnp.int32, (LANES, LANES), 1)
    for h in range(heads):
        for j in range(span // LANES):
            tall = cols_ref[pl.ds(j * LANES * heads + h, LANES, stride=heads), :]
            log_ref[h : h + 1, j * LANES : (j + 1) * LANES] = jnp.sum(
                jnp.where(eye, tall, 0.0), axis=0, keepdims=True
            )


def place(s, z, c):
    return (s * 2 + z) * 2 + c


def permuted(value, source):
    pairs = []
    for s in range(GROUP):
        for z in range(2):
            for c in range(2):
                at = source(s, z, c)
                if at is not None and at[0] >= 0:
                    pairs.append((place(*at), place(s, z, c)))
    return lax.ppermute(value, ("s", "z", "c"), pairs)


def per_device(queries, keys_values, doc_start):
    span, heads, width = queries.shape
    count = span * heads
    scale = width ** (-0.5)
    flat_q = queries.reshape(count, width)
    starts = doc_start.reshape(span // LANES, LANES)

    state = (
        jax.ShapeDtypeStruct((count, LANES), jnp.float32),
        jax.ShapeDtypeStruct((count, 2 * width), jnp.float32),
    )
    smem = pl.BlockSpec(memory_space=pltpu.SMEM)
    vmem = pl.BlockSpec(memory_space=pltpu.VMEM)
    params = pltpu.CompilerParams(vmem_limit_bytes=32 * 1024 * 1024)

    far = permuted(keys_values, lambda s, z, c: (s - 2, z, c))
    own = lax.all_gather(keys_values, ("z", "c"), axis=0)
    own, far = lax.optimization_barrier((own, far))
    near = permuted(own, lambda s, z, c: (s - 1, z, c) if c == 0 else (s - 3, z, c))
    far = lax.all_gather(far, "c", axis=0)
    over = permuted(far, lambda s, z, c: (s, 1 - z, c) if s >= 2 else None)
    starts, far = lax.optimization_barrier((starts, far))
    cols, first = pl.pallas_call(
        functools.partial(starts_kernel, heads),
        out_shape=(state[0], jax.ShapeDtypeStruct((4,), jnp.int32)),
        in_specs=[vmem],
        out_specs=(vmem, smem),
        compiler_params=params,
        cost_estimate=pl.CostEstimate(flops=400_000_000, bytes_accessed=1_000_000, transcendentals=0),
    )(starts)
    peak, acc = pl.pallas_call(
        functools.partial(own_kernel, heads, scale),
        out_shape=state,
        in_specs=[vmem, vmem, vmem],
        out_specs=(vmem, vmem),
        compiler_params=params,
        cost_estimate=pl.CostEstimate(flops=600_000_000, bytes_accessed=4_000_000, transcendentals=700_000),
    )(cols, flat_q, own)
    near = lax.all_gather(near, "c", axis=0)
    out, log_total = pl.pallas_call(
        functools.partial(earlier_kernel, heads, row_blocks(count), scale),
        out_shape=(
            jax.ShapeDtypeStruct((count, width), jnp.bfloat16),
            jax.ShapeDtypeStruct((heads, span), jnp.float32),
        ),
        in_specs=[smem] + [vmem] * 6,
        out_specs=(vmem,) * 2,
        scratch_shapes=[pltpu.VMEM((count, LANES), jnp.float32)],
        compiler_params=params,
        cost_estimate=pl.CostEstimate(flops=4_000_000_000, bytes_accessed=6_000_000, transcendentals=4_000_000),
    )(first, flat_q, far, over, near, peak, acc)
    return out.reshape(span, heads, width), log_total


def solution(mesh):
    grid = mesh.devices.reshape(-1, GROUP, 2, 2)
    return jax.shard_map(
        per_device,
        mesh=Mesh(grid, ("g", "s", "z", "c")),
        in_specs=(P(("g", "s"), ("z", "c"), None), P(None, ("g", "s", "z", "c"), None), P(("g", "s"))),
        out_specs=(P(("g", "s"), ("z", "c"), None), P(("z", "c"), ("g", "s"))),
        check_vma=False,
    )
```
